32 devices in a mesh: row: 4 (over y, x), col: 8 (over z, core).
Axes of the slice: x: 2, y: 2, z: 4, core: 2. Of those that a mesh axis runs over, the one named last changes fastest.
Arguments:
- operator: float32 [24576, 24576], P('row', 'col'), may hold values from -0.0546875 to 0.0546875
- modes: float32 [16, 84, 24576], P(None, None, ('col', 'row')), may hold values from -6 to 6
- coupling: float32 [84, 84], replicated, may hold values from -0.625 to 0.625
Outputs:
- mixed: float32 [16, 84, 24576], P(None, None, ('row', 'col'))
The draws below stay inside these ranges and needn't reach their ends.
All inputs are finite; a program needn't handle non-finite values.
Results may differ from the reference program's by a relative error of at most 0.000071.
Values sent between devices are 32-bit elements; how exact they have to be, the bound alone decides.
No kernel may reach another device: no remote copies, remote signals or barrier semaphores. Data moves between devices by JAX's collectives and lax.ppermute only.
A program may use at most 192 MiB of HBM per device.

```python
import jax
import jax.numpy as jnp
from jax import lax

N = 24576
P_SIZE = 84
CASES = 16


def raised(result, stream_key, source, target, blocks, factor):
    def block_of(dim):
        return (jnp.arange(result.shape[dim]) // (result.shape[dim] // blocks)).reshape((-1,) + (1,) * (result.ndim - 1 - dim))

    near = jax.random.permutation(stream_key, blocks)[block_of(target)]
    other_side = (block_of(target) + blocks // 2) % blocks
    return jnp.where((block_of(source) == near) | (block_of(source) == other_side), factor * result, result)


def steps_of(key, extent, pieces, low, largest):
    factor_of, own = 1.0, jax.random.fold_in(key, 6)
    for position, shards_of in pieces:
        steps = jnp.exp(jax.random.uniform(jax.random.fold_in(own, position), (shards_of,), jnp.float32, low / len(pieces), largest / len(pieces)))
        factor_of = factor_of * jnp.repeat(steps, extent[position] // shards_of).reshape([-1 if axis == position else 1 for axis in range(len(extent))])
    return factor_of


def centred(stream_key, dims, spread, most, pieces=(), dtype=jnp.bfloat16):
    gain = steps_of(stream_key, dims, pieces, -0.22, 0.18) if pieces else 1.0
    entries = jax.random.normal(stream_key, dims, jnp.float32) * spread * gain
    return jnp.minimum(jnp.maximum(entries, -most), most).astype(dtype)


def gaussian_with(key, dims, spread, reach, pieces, heavy, kind=jnp.bfloat16):
    values = spread * jax.random.normal(key, dims, jnp.float32)
    if pieces:
        values = values * steps_of(key, dims, pieces, -0.22, 0.18)
    return jnp.clip(raised(values, jax.random.fold_in(key, 3), *heavy), -reach, reach).astype(kind)


def setup_inputs(seed: int = 0) -> dict:
    seeds = jax.random.split(jax.random.key(seed), 4)
    return {
        "operator": gaussian_with(seeds[0], (N, N), N ** -0.5, 0.0546875, ((0, 4), (1, 8)), (1, 0, 8, 2.0), jnp.float32),
        "modes": centred(seeds[1], (CASES, P_SIZE, N), 1.0, 6.0, ((2, 32),), jnp.float32),
        "coupling": centred(seeds[2], (P_SIZE, P_SIZE), P_SIZE ** -0.5, 0.625, (), jnp.float32),
    }


def reference(operator, modes, coupling):
    flattened = modes.reshape(CASES * P_SIZE, N)
    applied = lax.dot_general(flattened, operator, (((1,), (1,)), ((), ())), precision=lax.Precision.HIGHEST, preferred_element_type=jnp.float32)
    applied = applied.reshape(CASES, P_SIZE, N)
    return jnp.einsum("pq,kqi->kpi", coupling, applied, precision=lax.Precision.HIGHEST)
```

```python
import functools

import jax
import jax.numpy as jnp
from jax import lax
from jax.experimental import pallas as pl
from jax.experimental.pallas import tpu as pltpu
from jax.sharding import PartitionSpec as P

CUTS = (0.131, 0.31, 0.607)
F32, BF16 = jnp.float32, jnp.bfloat16
LAST = (((1,), (1,)), ((), ()))
FIRST = (((1,), (0,)), ((), ()))
PARAMS = pltpu.CompilerParams(vmem_limit_bytes=64 * 2**20)
HBM = pl.BlockSpec(memory_space=pltpu.HBM)


def shares(count):
    cuts = [0] + [round(count * c) for c in CUTS] + [count]
    return [b - a for a, b in zip(cuts, cuts[1:])]


def halves(x):
    high = x.astype(BF16)
    return high, (x - high.astype(F32)).astype(BF16)


def dot(a, b, dims=LAST):
    return lax.dot_general(a, b, dims, preferred_element_type=F32)


def cost(products):
    return pl.CostEstimate(flops=6 * products, bytes_accessed=0, transcendentals=0)


def product_kernel(pieces, n_deps, where_ref, at_ref, *refs):
    parts, op_ref = refs[:pieces], refs[pieces]
    out_ref, split = refs[pieces + 1 + n_deps :]
    rows = parts[0].shape[1]

    @pl.when(pl.program_id(0) == 0)
    def _():
        for n, part in enumerate(parts):
            width = part.shape[2]
            for r in range(part.shape[0]):
                high, low = halves(part[r])
                start = r * width if pieces == 1 else pl.multiple_of(at_ref[n], 128)
                split[:rows, pl.ds(start, width)] = high
                split[rows:, pl.ds(start, width)] = low

    high, low = halves(op_ref[...])
    both = dot(split[...], high)
    out_ref[0] = both[:rows] + (both[rows:] + dot(split[:rows], low))


def product(parts, at, operator, width, where, deps=()):
    nb, rows, depth = where.shape[0], parts[0].shape[1], operator.shape[1]
    in_specs = [pl.BlockSpec(p.shape, lambda i, w, a: (0, 0, 0), pipeline_mode=pl.Buffered(1)) for p in parts]
    in_specs.append(pl.BlockSpec((width, depth), lambda i, w, a: (w[i], 0)))
    return pl.pallas_call(
        functools.partial(product_kernel, len(parts), len(deps)),
        grid_spec=pltpu.PrefetchScalarGridSpec(
            num_scalar_prefetch=2,
            grid=(nb,),
            in_specs=in_specs + [HBM] * len(deps),
            out_specs=pl.BlockSpec((1, rows, width), lambda i, w, a: (i, 0, 0)),
            scratch_shapes=[pltpu.VMEM((2 * rows, depth), BF16)],
        ),
        out_shape=jax.ShapeDtypeStruct((nb, rows, width), F32),
        compiler_params=PARAMS,
        cost_estimate=cost(nb * rows * width * depth),
        name="product",
    )(where, at, *parts, operator, *deps)


def mix_kernel(groups, cut, coupling_ref, x_ref, *refs):
    outs = refs[-len(groups) * cut :]
    count, cases, width = x_ref.shape
    x_high, x_low = halves(x_ref[...].reshape(count * cases, width))
    shape = (count, count * cases)
    spread = lax.broadcasted_iota(jnp.int32, shape, 1) // cases == lax.broadcasted_iota(jnp.int32, shape, 0)
    shape = (cases, count * cases)
    own = lax.broadcasted_iota(jnp.int32, shape, 1) % cases == lax.broadcasted_iota(jnp.int32, shape, 0)
    wide = lax.dot_general(
        coupling_ref[...], spread.astype(F32), FIRST, precision=lax.Precision.HIGHEST, preferred_element_type=F32
    )
    part = width // cut
    for n, (first, held) in enumerate(groups):
        rows = [jnp.where(own, jnp.broadcast_to(wide[p : p + 1], shape), 0.0) for p in range(first, first + held)]
        high, low = halves(jnp.concatenate(rows, 0))
        mixed = dot(high, x_high, FIRST) + (dot(high, x_low, FIRST) + dot(low, x_high, FIRST))
        for h in range(cut):
            outs[n * cut + h][0] = mixed[:, h * part : (h + 1) * part]


def mix(coupling, modes, groups, cut, deps=()):
    count, cases, width = modes.shape
    shapes = [(1, held * cases, width // cut) for _, held in groups for _ in range(cut)]
    return pl.pallas_call(
        functools.partial(mix_kernel, groups, cut),
        grid=(1,),
        in_specs=[pl.BlockSpec(coupling.shape, lambda i: (0, 0)), pl.BlockSpec(modes.shape, lambda i: (0, 0, 0))]
        + [HBM] * len(deps),
        out_specs=[pl.BlockSpec(shape, lambda i: (0, 0, 0)) for shape in shapes],
        out_shape=[jax.ShapeDtypeStruct(shape, F32) for shape in shapes],
        compiler_params=PARAMS,
        cost_estimate=cost(0),
        name="mix",
    )(coupling, modes, *deps)


def place_kernel(first, x_ref, *refs):
    out_ref, done = refs[-2:]
    copy = pltpu.make_async_copy(x_ref, out_ref.at[pl.ds(first, x_ref.shape[0])], done)
    copy.start()
    copy.wait()


def place(x, shape, first, out):
    extra = [] if out is None else [out]
    return pl.pallas_call(
        functools.partial(place_kernel, first),
        grid=(1,),
        in_specs=[pl.BlockSpec(x.shape, lambda i: (0, 0, 0))] + [HBM] * len(extra),
        out_specs=HBM,
        out_shape=jax.ShapeDtypeStruct(shape, F32),
        scratch_shapes=[pltpu.SemaphoreType.DMA],
        input_output_aliases={1: 0} if extra else {},
        compiler_params=PARAMS,
        name="place",
    )(x, *extra)


def per_device(sizes, operator, modes, coupling):
    modes = jnp.transpose(modes, (1, 0, 2))
    count, cases, width = modes.shape
    n_row, n_col = lax.axis_size("row"), lax.axis_size("col")
    row, core = lax.axis_index("row"), lax.axis_index("col") % 2
    chips = jnp.arange(n_col // 2, dtype=jnp.int32)
    theirs, mine = chips * 2 + (1 - core), chips * 2 + core
    line = [list(range(c, n_col, 2)) for c in range(2)]
    cores = [(c, c ^ 1) for c in range(n_col)]
    starts = [sum(sizes[:g]) for g in range(len(sizes))]
    n, half, send = len(sizes), width // 2, lax.ppermute
    square = n_row == 4 and half % 128 == 0
    along_x = [(r, r ^ 1) for r in range(n_row)]
    along_y = [(r, r ^ 2) for r in range(n_row)]
    token, parts, sums, out = (), {}, {}, None
    at = jnp.stack([(row ^ f) * width + h * half for f in range(4) for h in range(2)]).astype(jnp.int32)

    def gather(groups, deps=()):
        nonlocal token
        mixed = mix(coupling, modes, [(starts[g], sizes[g]) for g in groups], 1, (*token, *deps))
        token = (mixed[0],)
        for g, chunk in zip(groups, mixed):
            parts[g] = [lax.all_gather(chunk, "row", axis=0 if square else 2, tiled=True)]

    def gather_first():
        nonlocal token
        left, right = mix(coupling, modes, [(0, sizes[0])], 2)
        token = (right,)
        xl, yr = send(left, "row", along_x), send(right, "row", along_y)
        xr, yl = send(right, "row", along_x), send(left, "row", along_y)
        dl, dr = send(xl, "row", along_y), send(yr, "row", along_x)
        parts[0] = [left, right, xl, xr, yl, yr, dl, dr]
        return xl, yr, xr, yl

    def run(g, where):
        nonlocal token
        x = product(parts[g], at, operator, width, where, token)
        token = (x,)
        return x

    if square:
        hops = gather_first()
        gather(range(1, 2), hops)
    else:
        gather(range(n))
    for g in range(n):
        ex = send(run(g, theirs), "col", cores)
        if g == 0 and square:
            gather(range(2, n))
        total = run(g, mine) + ex
        token = (total,)
        sums[g] = lax.psum_scatter(total, "col", scatter_dimension=0, axis_index_groups=line)
    for g in range(n):
        out = place(sums[g].reshape(sizes[g], cases, width), (count, cases, width), starts[g], out)
    return jnp.transpose(out, (1, 0, 2))


def solution(mesh):
    def on_each(operator, modes, coupling):
        return per_device(shares(coupling.shape[0]), operator, modes, coupling)

    in_specs = (P("row", "col"), P(None, None, ("col", "row")), P())
    out_specs = P(None, None, ("row", "col"))
    return jax.shard_map(on_each, mesh=mesh, in_specs=in_specs, out_specs=out_specs, check_vma=False)
```

```python
import functools

import jax
import jax.numpy as jnp
from jax import lax
from jax.experimental import pallas as pl
from jax.experimental.pallas import tpu as pltpu
from jax.sharding import PartitionSpec as P

CUTS = (0.155, 0.36, 0.63)
F32, BF16 = jnp.float32, jnp.bfloat16
LAST = (((1,), (1,)), ((), ()))
FIRST = (((1,), (0,)), ((), ()))
PARAMS = pltpu.CompilerParams(vmem_limit_bytes=64 * 2**20)
HBM = pl.BlockSpec(memory_space=pltpu.HBM)


def shares(count):
    cuts = [0] + [round(count * c) for c in CUTS] + [count]
    return [b - a for a, b in zip(cuts, cuts[1:])]


def halves(x):
    high = x.astype(BF16)
    return high, (x - high.astype(F32)).astype(BF16)


def dot(a, b, dims=LAST):
    return lax.dot_general(a, b, dims, preferred_element_type=F32)


def cost(products):
    return pl.CostEstimate(flops=6 * products, bytes_accessed=0, transcendentals=0)


def product_kernel(pieces, n_deps, where_ref, at_ref, *refs):
    parts, op_ref = refs[:pieces], refs[pieces]
    out_ref, split = refs[pieces + 1 + n_deps :]
    rows = parts[0].shape[1]

    @pl.when(pl.program_id(0) == 0)
    def _():
        for n, part in enumerate(parts):
            width = part.shape[2]
            for r in range(part.shape[0]):
                high, low = halves(part[r])
                start = r * width if pieces == 1 else pl.multiple_of(at_ref[n], 128)
                split[:rows, pl.ds(start, width)] = high
                split[rows:, pl.ds(start, width)] = low

    high, low = halves(op_ref[...])
    both = dot(split[...], high)
    out_ref[0] = both[:rows] + (both[rows:] + dot(split[:rows], low))


def product(parts, at, operator, width, where, deps=()):
    nb, rows, depth = where.shape[0], parts[0].shape[1], operator.shape[1]
    in_specs = [pl.BlockSpec(p.shape, lambda i, w, a: (0, 0, 0), pipeline_mode=pl.Buffered(1)) for p in parts]
    in_specs.append(pl.BlockSpec((width, depth), lambda i, w, a: (w[i], 0)))
    return pl.pallas_call(
        functools.partial(product_kernel, len(parts), len(deps)),
        grid_spec=pltpu.PrefetchScalarGridSpec(
            num_scalar_prefetch=2,
            grid=(nb,),
            in_specs=in_specs + [HBM] * len(deps),
            out_specs=pl.BlockSpec((1, rows, width), lambda i, w, a: (i, 0, 0)),
            scratch_shapes=[pltpu.VMEM((2 * rows, depth), BF16)],
        ),
        out_shape=jax.ShapeDtypeStruct((nb, rows, width), F32),
        compiler_params=PARAMS,
        cost_estimate=cost(nb * rows * width * depth),
        name="product",
    )(where, at, *parts, operator, *deps)


def mix_kernel(groups, cut, coupling_ref, x_ref, *refs):
    outs = refs[-len(groups) * cut :]
    count, cases, width = x_ref.shape
    x_high, x_low = halves(x_ref[...].reshape(count * cases, width))
    shape = (count, count * cases)
    spread = lax.broadcasted_iota(jnp.int32, shape, 1) // cases == lax.broadcasted_iota(jnp.int32, shape, 0)
    shape = (cases, count * cases)
    own = lax.broadcasted_iota(jnp.int32, shape, 1) % cases == lax.broadcasted_iota(jnp.int32, shape, 0)
    wide = lax.dot_general(
        coupling_ref[...], spread.astype(F32), FIRST, precision=lax.Precision.HIGHEST, preferred_element_type=F32
    )
    part = width // cut
    for n, (first, held) in enumerate(groups):
        rows = [jnp.where(own, jnp.broadcast_to(wide[p : p + 1], shape), 0.0) for p in range(first, first + held)]
        high, low = halves(jnp.concatenate(rows, 0))
        mixed = dot(high, x_high, FIRST) + (dot(high, x_low, FIRST) + dot(low, x_high, FIRST))
        for h in range(cut):
            outs[n * cut + h][0] = mixed[:, h * part : (h + 1) * part]


def mix(coupling, modes, groups, cut, deps=()):
    count, cases, width = modes.shape
    shapes = [(1, held * cases, width // cut) for _, held in groups for _ in range(cut)]
    return pl.pallas_call(
        functools.partial(mix_kernel, groups, cut),
        grid=(1,),
        in_specs=[pl.BlockSpec(coupling.shape, lambda i: (0, 0)), pl.BlockSpec(modes.shape, lambda i: (0, 0, 0))]
        + [HBM] * len(deps),
        out_specs=[pl.BlockSpec(shape, lambda i: (0, 0, 0)) for shape in shapes],
        out_shape=[jax.ShapeDtypeStruct(shape, F32) for shape in shapes],
        compiler_params=PARAMS,
        cost_estimate=cost(sum(held for _, held in groups) * cases * count * cases * width),
        name="mix",
    )(coupling, modes, *deps)


def gate_kernel(*refs):
    del refs


def gate(arrays, deps):
    n = len(arrays)
    return pl.pallas_call(
        gate_kernel,
        in_specs=[HBM] * (n + len(deps)),
        out_specs=[HBM] * n,
        out_shape=[jax.ShapeDtypeStruct(x.shape, x.dtype) for x in arrays],
        input_output_aliases={i: i for i in range(n)},
        compiler_params=PARAMS,
        cost_estimate=cost(0),
        name="gate",
    )(*arrays, *deps)


def place_kernel(first, x_ref, *refs):
    out_ref, done = refs[-2:]
    copy = pltpu.make_async_copy(x_ref, out_ref.at[pl.ds(first, x_ref.shape[0])], done)
    copy.start()
    copy.wait()


def place(x, shape, first, out):
    extra = [] if out is None else [out]
    return pl.pallas_call(
        functools.partial(place_kernel, first),
        grid=(1,),
        in_specs=[pl.BlockSpec(x.shape, lambda i: (0, 0, 0))] + [HBM] * len(extra),
        out_specs=HBM,
        out_shape=jax.ShapeDtypeStruct(shape, F32),
        scratch_shapes=[pltpu.SemaphoreType.DMA],
        input_output_aliases={1: 0} if extra else {},
        compiler_params=PARAMS,
        name="place",
    )(x, *extra)


def per_device(sizes, operator, modes, coupling):
    modes = jnp.transpose(modes, (1, 0, 2))
    count, cases, width = modes.shape
    n_row, n_col = lax.axis_size("row"), lax.axis_size("col")
    row, core = lax.axis_index("row"), lax.axis_index("col") % 2
    chips = jnp.arange(n_col // 2, dtype=jnp.int32)
    theirs, mine = chips * 2 + (1 - core), chips * 2 + core
    line = [list(range(c, n_col, 2)) for c in range(2)]
    cores = [(c, c ^ 1) for c in range(n_col)]
    starts = [sum(sizes[:g]) for g in range(len(sizes))]
    n, half, send = len(sizes), width // 2, lax.ppermute
    square = n_row == 4 and half % 128 == 0
    along_x = [(r, r ^ 1) for r in range(n_row)]
    along_y = [(r, r ^ 2) for r in range(n_row)]
    token, parts, sums, out = (), {}, {}, None
    at = jnp.stack([(row ^ f) * width + h * half for f in range(4) for h in range(2)]).astype(jnp.int32)

    def mixed(groups):
        chunks = mix(coupling, modes, [(starts[g], sizes[g]) for g in groups], 1, token)
        return dict(zip(groups, chunks))

    def gather(chunks, deps):
        nonlocal token
        gated = gate(list(chunks.values()), (*token, *deps))
        token = (gated[0],)
        for g, chunk in zip(chunks, gated):
            parts[g] = [lax.all_gather(chunk, "row", axis=0 if square else 2, tiled=True)]

    def gather_first():
        nonlocal token
        left, right = mix(coupling, modes, [(0, sizes[0])], 2)
        token = (right,)
        xl, yr = send(left, "row", along_x), send(right, "row", along_y)
        xr, yl = send(right, "row", along_x), send(left, "row", along_y)
        dl, dr = send(xl, "row", along_y), send(yr, "row", along_x)
        parts[0] = [left, right, xl, xr, yl, yr, dl, dr]
        return xl, yr, xr, yl

    def run(g, where):
        nonlocal token
        x = product(parts[g], at, operator, width, where, token)
        token = (x,)
        return x

    if square:
        hops = gather_first()
        chunks = mixed(range(1, n))
        gather({g: chunks[g] for g in (1,)}, hops)
    else:
        gather(mixed(range(n)), ())
    for g in range(n):
        ex = send(run(g, theirs), "col", cores)
        if g == 0 and square:
            gather({g: chunks[g] for g in range(2, n)}, ())
        total = run(g, mine) + ex
        token = (total,)
        sums[g] = lax.psum_scatter(total, "col", scatter_dimension=0, axis_index_groups=line)
    for g in range(n):
        out = place(sums[g].reshape(sizes[g], cases, width), (count, cases, width), starts[g], out)
    return jnp.transpose(out, (1, 0, 2))


def solution(mesh):
    def on_each(operator, modes, coupling):
        return per_device(shares(coupling.shape[0]), operator, modes, coupling)

    in_specs = (P("row", "col"), P(None, None, ("col", "row")), P())
    out_specs = P(None, None, ("row", "col"))
    return jax.shard_map(on_each, mesh=mesh, in_specs=in_specs, out_specs=out_specs, check_vma=False)
```

```python
import functools

import jax
import jax.numpy as jnp
from jax import lax
from jax.experimental import pallas as pl
from jax.experimental.pallas import tpu as pltpu
from jax.sharding import PartitionSpec as P

CUTS = (0.155, 0.37, 0.643)
F32, BF16 = jnp.float32, jnp.bfloat16
LAST = (((1,), (1,)), ((), ()))
FIRST = (((1,), (0,)), ((), ()))
PARAMS = pltpu.CompilerParams(vmem_limit_bytes=64 * 2**20)
HBM = pl.BlockSpec(memory_space=pltpu.HBM)


def shares(count):
    cuts = [0] + [round(count * c) for c in CUTS] + [count]
    return [b - a for a, b in zip(cuts, cuts[1:])]


def halves(x):
    high = x.astype(BF16)
    return high, (x - high.astype(F32)).astype(BF16)


def dot(a, b, dims=LAST):
    return lax.dot_general(a, b, dims, preferred_element_type=F32)


def cost(products):
    return pl.CostEstimate(flops=6 * products, bytes_accessed=0, transcendentals=0)


def product_kernel(pieces, n_deps, where_ref, at_ref, *refs):
    parts, op_ref = refs[:pieces], refs[pieces]
    out_ref, split = refs[pieces + 1 + n_deps :]
    rows = parts[0].shape[1]

    @pl.when(pl.program_id(0) == 0)
    def _():
        for n, part in enumerate(parts):
            width = part.shape[2]
            for r in range(part.shape[0]):
                high, low = halves(part[r])
                start = r * width if pieces == 1 else pl.multiple_of(at_ref[n], 128)
                split[:rows, pl.ds(start, width)] = high
                split[rows:, pl.ds(start, width)] = low

    high, low = halves(op_ref[...])
    both = dot(split[...], high)
    out_ref[0] = both[:rows] + (both[rows:] + dot(split[:rows], low))


def product(parts, at, operator, width, where, deps=()):
    nb, rows, depth = where.shape[0], parts[0].shape[1], operator.shape[1]
    in_specs = [pl.BlockSpec(p.shape, lambda i, w, a: (0, 0, 0), pipeline_mode=pl.Buffered(1)) for p in parts]
    in_specs.append(pl.BlockSpec((width, depth), lambda i, w, a: (w[i], 0)))
    return pl.pallas_call(
        functools.partial(product_kernel, len(parts), len(deps)),
        grid_spec=pltpu.PrefetchScalarGridSpec(
            num_scalar_prefetch=2,
            grid=(nb,),
            in_specs=in_specs + [HBM] * len(deps),
            out_specs=pl.BlockSpec((1, rows, width), lambda i, w, a: (i, 0, 0)),
            scratch_shapes=[pltpu.VMEM((2 * rows, depth), BF16)],
        ),
        out_shape=jax.ShapeDtypeStruct((nb, rows, width), F32),
        compiler_params=PARAMS,
        cost_estimate=cost(nb * rows * width * depth),
        name="product",
    )(where, at, *parts, operator, *deps)


def mix_kernel(groups, cut, coupling_ref, x_ref, *refs):
    outs = refs[-len(groups) * cut :]
    count, cases, width = x_ref.shape
    x_high, x_low = halves(x_ref[...].reshape(count * cases, width))
    shape = (count, count * cases)
    spread = lax.broadcasted_iota(jnp.int32, shape, 1) // cases == lax.broadcasted_iota(jnp.int32, shape, 0)
    shape = (cases, count * cases)
    own = lax.broadcasted_iota(jnp.int32, shape, 1) % cases == lax.broadcasted_iota(jnp.int32, shape, 0)
    wide = lax.dot_general(
        coupling_ref[...], spread.astype(F32), FIRST, precision=lax.Precision.HIGHEST, preferred_element_type=F32
    )
    part = width // cut
    for n, (first, held) in enumerate(groups):
        rows = [jnp.where(own, jnp.broadcast_to(wide[p : p + 1], shape), 0.0) for p in range(first, first + held)]
        high, low = halves(jnp.concatenate(rows, 0))
        mixed = dot(high, x_high, FIRST) + (dot(high, x_low, FIRST) + dot(low, x_high, FIRST))
        for h in range(cut):
            outs[n * cut + h][0] = mixed[:, h * part : (h + 1) * part]


def mix(coupling, modes, groups, cut, deps=()):
    count, cases, width = modes.shape
    shapes = [(1, held * cases, width // cut) for _, held in groups for _ in range(cut)]
    return pl.pallas_call(
        functools.partial(mix_kernel, groups, cut),
        grid=(1,),
        in_specs=[pl.BlockSpec(coupling.shape, lambda i: (0, 0)), pl.BlockSpec(modes.shape, lambda i: (0, 0, 0))]
        + [HBM] * len(deps),
        out_specs=[pl.BlockSpec(shape, lambda i: (0, 0, 0)) for shape in shapes],
        out_shape=[jax.ShapeDtypeStruct(shape, F32) for shape in shapes],
        compiler_params=PARAMS,
        cost_estimate=cost(sum(held for _, held in groups) * cases * count * cases * width),
        name="mix",
    )(coupling, modes, *deps)


def gate_kernel(*refs):
    del refs


def gate(arrays, deps):
    n = len(arrays)
    return pl.pallas_call(
        gate_kernel,
        in_specs=[HBM] * (n + len(deps)),
        out_specs=[HBM] * n,
        out_shape=[jax.ShapeDtypeStruct(x.shape, x.dtype) for x in arrays],
        input_output_aliases={i: i for i in range(n)},
        compiler_params=PARAMS,
        cost_estimate=cost(0),
        name="gate",
    )(*arrays, *deps)


def place_kernel(first, x_ref, *refs):
    out_ref, done = refs[-2:]
    copy = pltpu.make_async_copy(x_ref, out_ref.at[pl.ds(first, x_ref.shape[0])], done)
    copy.start()
    copy.wait()


def place(x, shape, first, out):
    extra = [] if out is None else [out]
    return pl.pallas_call(
        functools.partial(place_kernel, first),
        grid=(1,),
        in_specs=[pl.BlockSpec(x.shape, lambda i: (0, 0, 0))] + [HBM] * len(extra),
        out_specs=HBM,
        out_shape=jax.ShapeDtypeStruct(shape, F32),
        scratch_shapes=[pltpu.SemaphoreType.DMA],
        input_output_aliases={1: 0} if extra else {},
        compiler_params=PARAMS,
        name="place",
    )(x, *extra)


def per_device(sizes, operator, modes, coupling):
    modes = jnp.transpose(modes, (1, 0, 2))
    count, cases, width = modes.shape
    n_row, n_col = lax.axis_size("row"), lax.axis_size("col")
    row, core = lax.axis_index("row"), lax.axis_index("col") % 2
    chips = jnp.arange(n_col // 2, dtype=jnp.int32)
    theirs, mine = chips * 2 + (1 - core), chips * 2 + core
    line = [list(range(c, n_col, 2)) for c in range(2)]
    cores = [(c, c ^ 1) for c in range(n_col)]
    starts = [sum(sizes[:g]) for g in range(len(sizes))]
    n, half, send = len(sizes), width // 2, lax.ppermute
    square = n_row == 4 and half % 128 == 0
    along_x = [(r, r ^ 1) for r in range(n_row)]
    along_y = [(r, r ^ 2) for r in range(n_row)]
    token, parts, sums, out = (), {}, {}, None
    at = jnp.stack([(row ^ f) * width + h * half for f in range(4) for h in range(2)]).astype(jnp.int32)

    def mixed(groups):
        chunks = mix(coupling, modes, [(starts[g], sizes[g]) for g in groups], 1, token)
        return dict(zip(groups, chunks))

    def gather(chunks, deps):
        nonlocal token
        gated = gate(list(chunks.values()), (*token, *deps))
        token = (gated[0],)
        for g, chunk in zip(chunks, gated):
            parts[g] = [lax.all_gather(chunk, "row", axis=0 if square else 2, tiled=True)]

    def gather_first():
        nonlocal token
        left, right = mix(coupling, modes, [(0, sizes[0])], 2)
        token = (right,)
        xl, yr = send(left, "row", along_x), send(right, "row", along_y)
        xr, yl = send(right, "row", along_x), send(left, "row", along_y)
        dl, dr = send(xl, "row", along_y), send(yr, "row", along_x)
        parts[0] = [left, right, xl, xr, yl, yr, dl, dr]
        return xl, yr, xr, yl

    def run(g, where):
        nonlocal token
        x = product(parts[g], at, operator, width, where, token)
        token = (x,)
        return x

    if square:
        hops = gather_first()
        chunks = mixed(range(1, n))
        gather({g: chunks[g] for g in (1,)}, hops)
    else:
        gather(mixed(range(n)), ())
    for g in range(n):
        if g == 0:
            every = run(g, jnp.arange(n_col, dtype=jnp.int32))
            if square:
                gather({g: chunks[g] for g in range(2, n)}, ())
            sums[g] = lax.psum_scatter(every, "col", scatter_dimension=0)
            continue
        ex = send(run(g, theirs), "col", cores)
        total = run(g, mine) + ex
        token = (total,)
        sums[g] = lax.psum_scatter(total, "col", scatter_dimension=0, axis_index_groups=line)
    for g in range(n):
        out = place(sums[g].reshape(sizes[g], cases, width), (count, cases, width), starts[g], out)
    return jnp.transpose(out, (1, 0, 2))


def solution(mesh):
    def on_each(operator, modes, coupling):
        return per_device(shares(coupling.shape[0]), operator, modes, coupling)

    in_specs = (P("row", "col"), P(None, None, ("col", "row")), P())
    out_specs = P(None, None, ("row", "col"))
    return jax.shard_map(on_each, mesh=mesh, in_specs=in_specs, out_specs=out_specs, check_vma=False)
```
